32 devices in a mesh: dp: 8 (over z, y), tensor: 4 (over x, core).
Axes of the slice: x: 2, y: 2, z: 4, core: 2. Of those that a mesh axis runs over, the one named last changes fastest.
Arguments:
- tokens: bfloat16 [16384, 1024], P(('dp', 'tensor')), may hold values from -6 to 6
- cotangent: bfloat16 [16384, 1024], P(('dp', 'tensor')), may hold values from -6 to 6
- segments: int32 [16384], P('dp'), may hold values from 0 to 15, never falling along the last dimension, each value on 1 to 1920 neighbouring positions
- routes: int32 [16384, 8], P(('dp', 'tensor')), may hold values from 0 to 31, all different within a row; in each aligned block of 512 rows (0 to 511, 512 to 1023, ...) at most 144 rows name the same one
- gain_attn: bfloat16 [1024], P(('dp', 'tensor')), may hold values from 0.5 to 1.5
- w_query: bfloat16 [1024, 1024], P('dp', 'tensor'), may hold values from -0.1875 to 0.1875
- key_weight: bfloat16 [1024, 512], P('dp', 'tensor'), may hold values from -0.1875 to 0.1875
- value_weight: bfloat16 [1024, 512], P('dp', 'tensor'), may hold values from -0.1875 to 0.1875
- w_out: bfloat16 [1024, 1024], P('tensor', 'dp'), may hold values from -0.75 to 0.75
- gain_moe: bfloat16 [1024], P(('dp', 'tensor')), may hold values from 0.5 to 1.5
- w_router: bfloat16 [1024, 32], P(('dp', 'tensor')), may hold values from -0.09375 to 0.09375
- w_gate: bfloat16 [32, 1024, 512], P('tensor', 'dp'), may hold values from -0.1875 to 0.1875
- w_up: bfloat16 [32, 1024, 512], P('tensor', 'dp'), may hold values from -0.1875 to 0.1875
- w_down: bfloat16 [32, 512, 1024], P('tensor', None, 'dp'), may hold values from -0.75 to 0.75
Outputs:
- mixed_out: bfloat16 [16384, 1024], P(('dp', 'tensor'))
- grad_tokens: float32 [16384, 1024], P(('dp', 'tensor'))
- grad_gain_attn: float32 [1024], P(('dp', 'tensor'))
- grad_w_query: float32 [1024, 1024], P('dp', 'tensor')
- grad_w_key: float32 [1024, 512], P('dp', 'tensor')
- grad_w_value: float32 [1024, 512], P('dp', 'tensor')
- grad_w_out: float32 [1024, 1024], P('tensor', 'dp')
- grad_gain_moe: float32 [1024], P(('dp', 'tensor'))
- grad_w_router: float32 [1024, 32], P(('dp', 'tensor'))
- grad_w_gate: float32 [32, 1024, 512], P('tensor', 'dp')
- grad_w_up: float32 [32, 1024, 512], P('tensor', 'dp')
- grad_w_down: float32 [32, 512, 1024], P('tensor', None, 'dp')
The draws below stay inside these ranges and needn't reach their ends.
Inputs may be any that keep to these rules, and one draw needn't show every extreme that they name: `segments`: segment numbers never fall along the tokens; a segment holds at most 1920 tokens, and one holds exactly that many. `routes`: each row names 8 different experts; in each aligned block of 512 rows (the rows of one device) no expert is named by more than 144 rows, a bound that some block reaches.
All inputs are finite; a program needn't handle non-finite values.
Results may differ from the reference program's by a relative error of at most 0.019.
Values may be sent and summed in bfloat16 or wider, within the bound.
A program may use at most 256 MiB of HBM per device.

```python
import math
import jax
import jax.numpy as jnp
import numpy as np
from jax import lax

MODEL_DIM = 1024
HQ = 16
KEY_VALUE_HEADS = 8
HEAD_DIM = 64
E = 32
FF = 512
TOPK = 8
SEQUENCE_LENGTH = 2048
GROUP_SEQUENCES = 1
GROUP_TOKENS = 2048
R = 512
CAP = 144
TOKENS = 16384
N_DP = 8
N_TENSOR = 4


def block_scale(rng, shape, split, least, largest):
    loudness = 1.0
    for axis_at, parts in split:
        draws = jax.random.uniform(jax.random.fold_in(jax.random.fold_in(rng, 6), axis_at), (parts,), jnp.float32, least / len(split), largest / len(split))
        loudness = loudness * jnp.repeat(jnp.exp(draws), shape[axis_at] // parts).reshape((-1,) + (1,) * (len(shape) - 1 - axis_at))
    return loudness


def length_profile(count, total, reach, lean):
    loads = [(1 << 20) // math.isqrt(rank ** lean) + 1 for rank in range(2, count + 1)]
    rest, counts = total - reach - (count - 1), [1] * (count - 1)
    while rest > 0:
        candidates = [i for i in range(count - 1) if counts[i] < reach]
        whole, left = sum([loads[i] for i in candidates]), rest
        for i in candidates:
            more = min(reach - counts[i], max(1, left * loads[i] // whole), rest)
            counts[i] = counts[i] + more
            rest = rest - more
    return np.array([reach] + counts)


def uneven_parts(own_key, number_of, total, most, skew):
    if number_of == 2:
        one = jax.random.randint(own_key, (), max(1, total - most), min(most, total - 1) + 1)
        return jnp.stack([one, total - one])
    tallies = jnp.asarray(length_profile(number_of, total, most, skew), jnp.int32)
    couples = (number_of - 1) // 2
    source_of, sink = tallies[1:1 + 2 * couples:2], tallies[2:2 + 2 * couples:2]
    slack = jnp.minimum(source_of - 1, most - sink)
    moved = jax.random.randint(jax.random.fold_in(own_key, 1), (couples,), 0, 1 << 20) % (slack + 1)
    tallies = tallies.at[1:1 + 2 * couples:2].set(source_of - moved).at[2:2 + 2 * couples:2].set(sink + moved)
    return tallies[jax.random.permutation(jax.random.fold_in(own_key, 2), number_of)]


def routed_block(rng, own, number, rows, number_of, top, bound, skew):
    sequence = jax.random.permutation(rng, number_of)
    heavy_load, common = portions_of(number_of, rows * top, bound, skew, True), portions_of(number_of, rows * top, bound, skew, False)
    places = jnp.arange(number_of)

    def named(sizes, turn):
        used = int((sizes > 0).sum())
        fixed = max(1, used // 4)
        moved = fixed + (places - fixed + turn * (used - fixed)) % max(1, number_of - fixed)
        return jnp.zeros((number_of,), jnp.int32).at[sequence[jnp.where(places < fixed, places, moved)]].set(jnp.asarray(sizes, jnp.int32))

    sizes = jnp.where(number % 4 == 0, named(heavy_load, number // 4), named(common, number - number // 4 - 1))
    mixed = jax.random.permutation(jax.random.fold_in(own, 3), number_of)
    source_of, sink = mixed[0:number_of // 2 * 2:2], mixed[1:number_of // 2 * 2:2]
    margin = jnp.minimum(sizes[source_of] - 1, bound - sizes[sink]) // 2
    margin = jnp.where((source_of == sequence[0]) | (sink == sequence[0]) | (sizes[sink] == 0), 0, jnp.maximum(margin, 0))
    moved = jax.random.randint(jax.random.fold_in(own, 4), (number_of // 2,), 0, 1 << 20) % (margin + 1)
    sizes = sizes.at[source_of].add(-moved).at[sink].add(moved)
    labels = jnp.searchsorted(jnp.cumsum(sizes), jnp.arange(rows * top), side="right").astype(jnp.int32)
    listing = labels.reshape(top, rows).T
    listing = listing[jax.random.permutation(jax.random.fold_in(own, 1), rows)]
    turn = jax.random.randint(jax.random.fold_in(own, 2), (rows, 1), 0, top)
    return jnp.take_along_axis(listing, (jnp.arange(top)[None, :] + turn) % top, axis=1)


def portions_of(count, total, limit, slope, full):
    loads = [(1 << 20) // math.isqrt(grade ** slope) + 1 for grade in range(1, count + 1)]
    largest = limit if full else min(limit, max(-(-total // count), total * loads[0] // sum(loads)))
    least = 1 if total - largest >= count - 1 else 0
    counts, surplus = [largest] + [least] * (count - 1), total - largest - least * (count - 1)
    while surplus > 0:
        candidates = [i for i in range(1, count) if counts[i] < largest] or [i for i in range(1, count) if counts[i] < limit]
        whole, left = sum([loads[i] for i in candidates]), surplus
        for i in candidates:
            extra = min(limit - counts[i], max(1, left * loads[i] // whole), surplus)
            counts[i] = counts[i] + extra
            surplus = surplus - extra
    return np.array(counts)


def noise(own_key, extent, scale, bound, shards=(), kind=jnp.bfloat16):
    level = block_scale(own_key, extent, shards, -0.22, 0.18) if shards else 1.0
    values = jax.random.normal(own_key, extent, jnp.float32) * scale * level
    return jnp.minimum(jnp.maximum(values, -bound), bound).astype(kind)


def setup_inputs(seed: int = 0) -> dict:
    streams_of = jax.random.split(jax.random.key(seed), 15)
    tokens = noise(streams_of[0], (TOKENS, MODEL_DIM), 1, 6.0, ((0, 32),))
    cotangent = noise(streams_of[1], (TOKENS, MODEL_DIM), 1, 6.0, ((0, 32),))
    segments = jnp.searchsorted(jnp.cumsum(uneven_parts(streams_of[2], 2 * TOKENS // SEQUENCE_LENGTH, TOKENS, SEQUENCE_LENGTH * 15 // 16, 1)), jnp.arange(TOKENS), side="right").astype(jnp.int32)
    routes_keys = jax.random.split(jax.random.fold_in(streams_of[3], 1), TOKENS // R)
    routes_turns = jax.random.permutation(jax.random.fold_in(streams_of[3], 3), TOKENS // R)
    routes = jax.vmap(lambda own, number: routed_block(jax.random.fold_in(streams_of[3], 2), own, number, R, E, TOPK, CAP, 1))(routes_keys, routes_turns).reshape((TOKENS, TOPK))
    gain_attn = jnp.clip(1.0 + 0.1 * jax.random.normal(streams_of[4], (MODEL_DIM,), jnp.float32), 0.5, 1.5).astype(jnp.bfloat16)
    w_query = noise(streams_of[5], (MODEL_DIM, HQ * HEAD_DIM), MODEL_DIM ** -0.5, 0.1875, ((0, 8), (1, 4)))
    key_weight = noise(streams_of[6], (MODEL_DIM, KEY_VALUE_HEADS * HEAD_DIM), MODEL_DIM ** -0.5, 0.1875, ((0, 8), (1, 4)))
    value_weight = noise(streams_of[7], (MODEL_DIM, KEY_VALUE_HEADS * HEAD_DIM), MODEL_DIM ** -0.5, 0.1875, ((0, 8), (1, 4)))
    w_out = noise(streams_of[8], (HQ * HEAD_DIM, MODEL_DIM), (HQ * HEAD_DIM // 16) ** -0.5, 0.75, ((0, 4), (1, 8)))
    gain_moe = jnp.clip(1.0 + 0.1 * jax.random.normal(streams_of[9], (MODEL_DIM,), jnp.float32), 0.5, 1.5).astype(jnp.bfloat16)
    w_router = noise(streams_of[10], (MODEL_DIM, E), (4 * MODEL_DIM) ** -0.5, 0.09375, ((0, 32),))
    w_gate = noise(streams_of[11], (E, MODEL_DIM, FF), MODEL_DIM ** -0.5, 0.1875, ((0, 4), (1, 8)))
    w_up = noise(streams_of[12], (E, MODEL_DIM, FF), MODEL_DIM ** -0.5, 0.1875, ((0, 4), (1, 8)))
    w_down = noise(streams_of[13], (E, FF, MODEL_DIM), (FF // 8) ** -0.5, 0.75, ((0, 4), (2, 8)))
    return dict(tokens=tokens, cotangent=cotangent, segments=segments, routes=routes, gain_attn=gain_attn, w_query=w_query, key_weight=key_weight, value_weight=value_weight, w_out=w_out, gain_moe=gain_moe, w_router=w_router, w_gate=w_gate, w_up=w_up, w_down=w_down)


HIGHEST = lax.Precision.HIGHEST
EPSILON = 1e-06
ROTARY_BASE = 10000.0
MASKED_SCORE = -1e+30

@jax.custom_vjp
def lower_precision(v):
    return lax.optimization_barrier(v.astype(jnp.bfloat16)).astype(jnp.float32)

@jax.custom_vjp
def lower_precision_back(v):
    return v

def low_keep(v):
    return (lower_precision(v), None)

def low_pass(kept, grad):
    return (grad,)

def back_keep(v):
    return (v, None)

def back_low(kept, grad):
    return (lower_precision(grad),)
lower_precision.defvjp(low_keep, low_pass)
lower_precision_back.defvjp(back_keep, back_low)

def dot_product(left, right):
    return jnp.dot(left, right, precision=HIGHEST, preferred_element_type=jnp.float32)

def rms_norm(values, gain):
    factor = lax.rsqrt(lax.optimization_barrier(jnp.mean(values * values, axis=-1, keepdims=True)) + EPSILON)
    return values * factor * gain

def positions_of(segment_rows):
    length = segment_rows.shape[1]
    place = jnp.arange(length, dtype=jnp.int32)
    shifted = jnp.concatenate([segment_rows[:, :1], segment_rows[:, :-1]], axis=1)
    opening = (place[None, :] == 0) | (segment_rows != shifted)
    begin = lax.cummax(jnp.where(opening, place[None, :], 0), axis=1)
    return place[None, :] - begin

def rotary_tables(position, head_size):
    half_size = head_size // 2
    frequency = jnp.exp(jnp.arange(half_size, dtype=jnp.float32) * (-2.0 * math.log(ROTARY_BASE) / head_size))
    angle = position.astype(jnp.float32)[:, None] * frequency[None, :]
    return (jnp.cos(angle), jnp.sin(angle))

def apply_rotary(values, cosine_table, sine_values):
    half_size = values.shape[-1] // 2
    front_half = values[..., :half_size]
    back_half = values[..., half_size:]
    cos_b = cosine_table[:, None, :]
    sin_b = sine_values[:, None, :]
    return jnp.concatenate([front_half * cos_b - back_half * sin_b, back_half * cos_b + front_half * sin_b], axis=-1)

def attend(inputs_seq):
    queries, key_matrix, value_matrix, segment_ids = inputs_seq
    length = queries.shape[0]
    kv_heads = key_matrix.shape[1]
    head_share = queries.shape[1] // kv_heads
    grouped = queries.reshape(length, kv_heads, head_share, queries.shape[2])
    raw_scores = jnp.einsum('qcgd,kcd->cgqk', grouped, key_matrix, precision=HIGHEST)
    raw_scores = lower_precision_back(raw_scores * queries.shape[2] ** (-0.5))
    place = jnp.arange(length)
    allowed = (segment_ids[:, None] == segment_ids[None, :]) & (place[None, :] <= place[:, None])
    masked = jnp.where(allowed, raw_scores, MASKED_SCORE)
    softmaxed = lower_precision(jax.nn.softmax(masked, axis=-1))
    result = jnp.einsum('cgqk,kcd->qcgd', softmaxed, value_matrix, precision=HIGHEST)
    return result.reshape(length, -1)

def expert(inputs_exp):
    batch_rows, gate_w, up_w, down_w = inputs_exp
    pre_gate = lower_precision_back(dot_product(batch_rows, gate_w))
    pre_up = lower_precision_back(dot_product(batch_rows, up_w))
    activation = lower_precision(jax.nn.silu(pre_gate) * pre_up)
    return lower_precision_back(lower_precision(dot_product(activation, down_w)))

def block_forward(inputs, segment_ids, route_rows, gain_attn, w_query, key_weight, value_weight, w_out, gain_moe, w_router, w_gate, w_up, w_down):
    normed_rows = lower_precision(rms_norm(inputs, gain_attn))
    query_lin = lower_precision_back(dot_product(normed_rows, w_query)).reshape(GROUP_TOKENS, HQ, HEAD_DIM)
    key_linear = lower_precision_back(dot_product(normed_rows, key_weight)).reshape(GROUP_TOKENS, KEY_VALUE_HEADS, HEAD_DIM)
    value_matrix = lower_precision_back(lower_precision(dot_product(normed_rows, value_weight))).reshape(GROUP_SEQUENCES, SEQUENCE_LENGTH, KEY_VALUE_HEADS, HEAD_DIM)
    segment_rows = segment_ids.reshape(GROUP_SEQUENCES, SEQUENCE_LENGTH)
    cosine_table, sine_values = rotary_tables(positions_of(segment_rows).reshape(GROUP_TOKENS), HEAD_DIM)
    queries = lower_precision(apply_rotary(query_lin, cosine_table, sine_values)).reshape(GROUP_SEQUENCES, SEQUENCE_LENGTH, HQ, HEAD_DIM)
    key_matrix = lower_precision(apply_rotary(key_linear, cosine_table, sine_values)).reshape(GROUP_SEQUENCES, SEQUENCE_LENGTH, KEY_VALUE_HEADS, HEAD_DIM)
    mixed = lax.map(jax.checkpoint(attend), (queries, key_matrix, value_matrix, segment_rows))
    mixed = lower_precision_back(lower_precision(mixed.reshape(GROUP_TOKENS, HQ * HEAD_DIM)))
    hidden = inputs + lower_precision_back(dot_product(mixed, w_out))
    normed_moe = lower_precision(rms_norm(hidden, gain_moe))
    logits = dot_product(normed_moe, w_router)
    gates = jax.nn.softmax(jnp.take_along_axis(logits, route_rows, axis=1), axis=-1)
    copies = lower_precision_back(jnp.broadcast_to(normed_moe[:, None, :], (GROUP_TOKENS, TOPK, MODEL_DIM))).reshape(GROUP_TOKENS * TOPK, MODEL_DIM)
    flat_routes = route_rows.reshape(N_TENSOR, R * TOPK)
    matches = (flat_routes[:, :, None] == jnp.arange(E, dtype=jnp.int32)[None, None, :]).astype(jnp.int32)
    slot_rank = lax.optimization_barrier(jnp.sum(matches * (jnp.cumsum(matches, axis=1, dtype=jnp.int32) - 1), axis=2, dtype=jnp.int32))
    source_block = jnp.arange(N_TENSOR, dtype=jnp.int32)[:, None]
    slot_of = (flat_routes * (N_TENSOR * CAP) + source_block * CAP + slot_rank).reshape(GROUP_TOKENS * TOPK)
    source = jnp.full((E * N_TENSOR * CAP,), GROUP_TOKENS * TOPK, jnp.int32).at[slot_of].set(jnp.arange(GROUP_TOKENS * TOPK, dtype=jnp.int32))
    padded = jnp.concatenate([copies, jnp.zeros((1, MODEL_DIM), copies.dtype)], axis=0)
    buffers = padded[source].reshape(E, N_TENSOR * CAP, MODEL_DIM)
    outputs = lax.map(jax.checkpoint(expert), (buffers, w_gate, w_up, w_down))
    returned = outputs.reshape(E * N_TENSOR * CAP, MODEL_DIM)[slot_of].reshape(GROUP_TOKENS, TOPK, MODEL_DIM)
    return hidden + lax.optimization_barrier(jnp.sum(gates[:, :, None] * returned, axis=1))

def reference(tokens, cotangent, segments, routes, gain_attn, w_query, key_weight, value_weight, w_out, gain_moe, w_router, w_gate, w_up, w_down):
    weights = tuple((item.astype(jnp.float32) for item in (gain_attn, w_query, key_weight, value_weight, w_out, gain_moe, w_router, w_gate, w_up, w_down)))
    segment_groups = segments.reshape(N_DP, GROUP_TOKENS)
    route_groups = routes.reshape(N_DP, GROUP_TOKENS, TOPK)

    def forward(inputs, *params):

        def one_group(group_args):
            group_inputs, group_segments, group_routes = group_args
            return block_forward(group_inputs, group_segments, group_routes, *params)
        stacked = lax.map(jax.checkpoint(one_group), (inputs.reshape(N_DP, GROUP_TOKENS, MODEL_DIM), segment_groups, route_groups))
        return stacked.reshape(N_DP * GROUP_TOKENS, MODEL_DIM)
    result, pullback = jax.vjp(forward, tokens.astype(jnp.float32), *weights)
    grads = pullback(cotangent.astype(jnp.float32))
    return (result.astype(jnp.bfloat16), grads[0], grads[1], grads[2], grads[3], grads[4], grads[5], grads[6], grads[7], grads[8], grads[9], grads[10])
```

```python
import functools
import math

import jax
import jax.numpy as jnp
from jax import lax
from jax.experimental import pallas as pl
from jax.experimental.pallas import tpu as pltpu
from jax.sharding import PartitionSpec as P

HEAD_DIM = 64
E = 32
TOPK = 8
SEQUENCE_LENGTH = 2048


HIGHEST = lax.Precision.HIGHEST
EPSILON = 1e-06
ROTARY_BASE = 10000.0
MASKED_SCORE = -1e30
BLOCK = 512
F32 = jnp.float32
BF16 = jnp.bfloat16


def rms_forward(values, gain):
    factor = lax.rsqrt(jnp.mean(values * values, axis=-1, keepdims=True) + EPSILON)
    return (values * factor * gain, factor)


def rms_backward(values, factor, gain, grad):
    normal = values * factor
    gain_grad = jnp.sum(grad * normal, axis=0)
    inner = grad * gain
    back = factor * (inner - normal * jnp.mean(inner * normal, axis=-1, keepdims=True))
    return (back, gain_grad)


def positions_of(segment_rows):
    length = segment_rows.shape[1]
    place = jnp.arange(length, dtype=jnp.int32)
    shifted = jnp.concatenate([segment_rows[:, :1], segment_rows[:, :-1]], axis=1)
    opening = (place[None, :] == 0) | (segment_rows != shifted)
    begin = lax.cummax(jnp.where(opening, place[None, :], 0), axis=1)
    return place[None, :] - begin


def rotary_tables(position, head_size):
    half_size = head_size // 2
    frequency = jnp.exp(
        jnp.arange(half_size, dtype=jnp.float32) * (-2.0 * math.log(ROTARY_BASE) / head_size)
    )
    angle = position.astype(jnp.float32)[:, None] * frequency[None, :]
    return (jnp.cos(angle), jnp.sin(angle))


def turn_heads(values, cosine_table, sine_values):
    half_size = values.shape[-1] // 2
    front_half = values[..., :half_size]
    back_half = values[..., half_size:]
    cos_b = cosine_table[None]
    sin_b = sine_values[None]
    return jnp.concatenate(
        [front_half * cos_b - back_half * sin_b, back_half * cos_b + front_half * sin_b], axis=-1
    )


def to_heads(values, heads):
    return values.reshape(values.shape[0], heads, HEAD_DIM).transpose(1, 0, 2)


def from_heads(values):
    return values.transpose(1, 0, 2).reshape(values.shape[1], -1)


def dot_nt(left, right):
    return lax.dot_general(left, right, (((1,), (1,)), ((), ())), preferred_element_type=F32)


def dot_tn(left, right):
    return lax.dot_general(left, right, (((0,), (0,)), ((), ())), preferred_element_type=F32)


def allowed_block(query_segments, key_segments, i, j, block):
    row = i * block + lax.broadcasted_iota(jnp.int32, (block, block), 0)
    column = j * block + lax.broadcasted_iota(jnp.int32, (block, block), 1)
    return (query_segments == key_segments) & (column <= row)


def attend_kernel(block, scale, q_ref, k_ref, v_ref, segq_ref, segk_ref, out_ref, total_ref):
    i = pl.program_id(1)
    queries = q_ref[0]
    query_segments = segq_ref[...]

    def step(j, carry):
        row_max, row_sum, mix = carry
        start = pl.multiple_of(j * block, block)
        scores = dot_nt(queries, k_ref[0, pl.ds(start, block), :]) * scale
        allowed = allowed_block(query_segments, segk_ref[j], i, j, block)
        scores = jnp.where(allowed, scores, MASKED_SCORE)
        new_max = jnp.maximum(row_max, jnp.max(scores, axis=-1, keepdims=True))
        weights = jnp.exp(scores - new_max)
        shrink = jnp.exp(row_max - new_max)
        row_sum = row_sum * shrink + jnp.sum(weights, axis=-1, keepdims=True)
        mix = mix * shrink + jnp.dot(
            weights.astype(BF16), v_ref[0, pl.ds(start, block), :], preferred_element_type=F32
        )
        return new_max, row_sum, mix

    row_max, row_sum, mix = lax.fori_loop(
        0,
        i + 1,
        step,
        (
            jnp.full((block, 1), MASKED_SCORE, F32),
            jnp.zeros((block, 1), F32),
            jnp.zeros((block, HEAD_DIM), F32),
        ),
    )
    out_ref[0] = (mix / row_sum).astype(BF16)
    total_ref[0] = row_max + jnp.log(row_sum)


def attend_forward(queries, keys, values, segments, scale):
    heads, length, _ = queries.shape
    share = heads // keys.shape[0]
    block = min(BLOCK, length)
    blocks = length // block
    return pl.pallas_call(
        functools.partial(attend_kernel, block, scale),
        grid=(heads, blocks),
        in_specs=[
            pl.BlockSpec((1, block, HEAD_DIM), lambda h, i: (h, i, 0)),
            pl.BlockSpec((1, length, HEAD_DIM), lambda h, i: (h // share, 0, 0)),
            pl.BlockSpec((1, length, HEAD_DIM), lambda h, i: (h // share, 0, 0)),
            pl.BlockSpec((block, 1), lambda h, i: (i, 0)),
            pl.BlockSpec((blocks, 1, block), lambda h, i: (0, 0, 0)),
        ],
        out_specs=[
            pl.BlockSpec((1, block, HEAD_DIM), lambda h, i: (h, i, 0)),
            pl.BlockSpec((1, block, 1), lambda h, i: (h, i, 0)),
        ],
        out_shape=[
            jax.ShapeDtypeStruct((heads, length, HEAD_DIM), BF16),
            jax.ShapeDtypeStruct((heads, length, 1), F32),
        ],
        compiler_params=pltpu.CompilerParams(vmem_limit_bytes=32 * 1024 * 1024),
        cost_estimate=pl.CostEstimate(
            flops=heads * length * length * HEAD_DIM * 3,
            bytes_accessed=heads * length * HEAD_DIM * 8,
            transcendentals=heads * length * length // 2,
        ),
    )(queries, keys, values, segments.reshape(length, 1), segments.reshape(blocks, 1, block))


def attend_back_kernel(
    block,
    scale,
    q_ref,
    k_ref,
    v_ref,
    grad_ref,
    mix_ref,
    total_ref,
    segq_ref,
    segk_ref,
    dq_ref,
    dk_ref,
    dv_ref,
):
    g = pl.program_id(1)
    i = pl.program_id(2)

    @pl.when((g == 0) & (i == 0))
    def _():
        dk_ref[...] = jnp.zeros_like(dk_ref)
        dv_ref[...] = jnp.zeros_like(dv_ref)

    queries = q_ref[0]
    grad = grad_ref[0]
    total = total_ref[0]
    query_segments = segq_ref[...]
    inner = jnp.sum(grad.astype(F32) * mix_ref[0].astype(F32), axis=-1, keepdims=True)

    def step(j, query_grad):
        start = pl.multiple_of(j * block, block)
        here = pl.ds(start, block)
        keys = k_ref[0, here, :]
        scores = dot_nt(queries, keys) * scale
        allowed = allowed_block(query_segments, segk_ref[j], i, j, block)
        softmaxed = jnp.exp(jnp.where(allowed, scores - total, MASKED_SCORE))
        prob_grad = dot_nt(grad, v_ref[0, here, :])
        score_grad = (softmaxed * (prob_grad - inner)).astype(BF16)
        dv_ref[0, here, :] += dot_tn(softmaxed.astype(BF16), grad)
        dk_ref[0, here, :] += dot_tn(score_grad, queries) * scale
        return query_grad + jnp.dot(score_grad, keys, preferred_element_type=F32)

    query_grad = lax.fori_loop(0, i + 1, step, jnp.zeros((block, HEAD_DIM), F32))
    dq_ref[0] = query_grad * scale


def attend_backward(queries, keys, values, segments, totals, mix, mix_grad, scale):
    heads, length, _ = queries.shape
    kv_heads = keys.shape[0]
    share = heads // kv_heads
    block = min(BLOCK, length)
    blocks = length // block
    by_query = pl.BlockSpec((1, block, HEAD_DIM), lambda c, g, i: (c * share + g, i, 0))
    by_key = pl.BlockSpec((1, length, HEAD_DIM), lambda c, g, i: (c, 0, 0))
    return pl.pallas_call(
        functools.partial(attend_back_kernel, block, scale),
        grid=(kv_heads, share, blocks),
        in_specs=[
            by_query,
            by_key,
            by_key,
            by_query,
            by_query,
            pl.BlockSpec((1, block, 1), lambda c, g, i: (c * share + g, i, 0)),
            pl.BlockSpec((block, 1), lambda c, g, i: (i, 0)),
            pl.BlockSpec((blocks, 1, block), lambda c, g, i: (0, 0, 0)),
        ],
        out_specs=[by_query, by_key, by_key],
        out_shape=[
            jax.ShapeDtypeStruct((heads, length, HEAD_DIM), F32),
            jax.ShapeDtypeStruct((kv_heads, length, HEAD_DIM), F32),
            jax.ShapeDtypeStruct((kv_heads, length, HEAD_DIM), F32),
        ],
        compiler_params=pltpu.CompilerParams(vmem_limit_bytes=32 * 1024 * 1024),
        cost_estimate=pl.CostEstimate(
            flops=heads * length * length * HEAD_DIM * 6,
            bytes_accessed=heads * length * HEAD_DIM * 24,
            transcendentals=heads * length * length // 2,
        ),
    )(
        queries,
        keys,
        values,
        mix_grad,
        mix,
        totals,
        segments.reshape(length, 1),
        segments.reshape(blocks, 1, block),
    )


def per_device(
    tokens,
    cotangent,
    segments,
    routes,
    gain_attn,
    w_query,
    key_weight,
    value_weight,
    w_out,
    gain_moe,
    w_router,
    w_gate,
    w_up,
    w_down,
):
    groups = lax.axis_size("tensor")
    copies = lax.axis_size("dp")
    member = lax.axis_index("tensor")
    row_total, width = tokens.shape
    length = segments.shape[0]
    scale = HEAD_DIM ** (-0.5)
    local_experts, part, hidden_units = w_gate.shape
    capacity = max(2, row_total * TOPK * 9 // (8 * E))
    gain_part = gain_attn.shape[0]
    q_width = w_query.shape[1]
    kv_width = key_weight.shape[1]
    q_heads = q_width // HEAD_DIM
    kv_heads = kv_width // HEAD_DIM

    route_size = row_total * TOPK
    out_size = w_out.size
    small_size = gain_part * (E + 2)
    extra = jnp.concatenate(
        [
            routes.astype(BF16).reshape(-1),
            w_out.T.reshape(-1),
            w_router.reshape(-1),
            gain_attn,
            gain_moe,
        ]
    )
    extra_rows = -(-extra.size // (16 * width)) * 16
    extra = jnp.pad(extra, (0, extra_rows * width - extra.size)).reshape(extra_rows, width)
    first = lax.all_gather(jnp.concatenate([tokens, cotangent, extra], axis=0), "tensor", axis=0)
    all_tokens = first[:, :row_total].reshape(length, width)
    all_cotangent = first[:, row_total : 2 * row_total].reshape(length, width)
    extras = first[:, 2 * row_total :].reshape(groups, extra_rows * width)
    all_routes = extras[:, :route_size].reshape(length, TOPK).astype(jnp.int32)
    out_block = extras[:, route_size : route_size + out_size].reshape(groups, part, q_width)
    out_block = out_block.transpose(1, 0, 2).reshape(part, groups * q_width)
    small = extras[:, route_size + out_size : route_size + out_size + small_size].reshape(-1)

    block = jnp.concatenate([w_query, key_weight, value_weight, out_block], axis=1)
    small_rows = -(-small.size // (16 * block.shape[1])) * 16
    small_block = jnp.pad(small, (0, small_rows * block.shape[1] - small.size))
    second = lax.all_gather(
        jnp.concatenate([block, small_block.reshape(small_rows, -1)], axis=0), "dp", axis=0
    )
    weights = second[:, :part].reshape(width, block.shape[1])
    qkv_width = q_width + 2 * kv_width
    qkv_w = weights[:, :qkv_width]
    out_w_t = weights[:, qkv_width:]
    smalls = second[:, part:].reshape(copies, -1)[:, : small.size].reshape(-1, small_size)
    router = smalls[:, : gain_part * E].reshape(width, E)
    gain_a = smalls[:, gain_part * E : gain_part * (E + 1)].reshape(width).astype(F32)
    gain_m = smalls[:, gain_part * (E + 1) :].reshape(width).astype(F32)

    gate_part, up_part, down_part, second = lax.optimization_barrier(
        (w_gate, w_up, w_down.transpose(0, 2, 1), second)
    )
    gate_w = lax.all_gather(gate_part, "dp", axis=1, tiled=True)
    up_w = lax.all_gather(up_part, "dp", axis=1, tiled=True)
    down_w = lax.all_gather(down_part, "dp", axis=1, tiled=True)

    inputs = all_tokens.astype(F32)
    normed, factor_a = rms_forward(inputs, gain_a)
    normed = normed.astype(BF16)
    cosine_table, sine_values = rotary_tables(
        positions_of(segments.reshape(-1, SEQUENCE_LENGTH)).reshape(length), HEAD_DIM
    )
    linear = jnp.dot(normed, qkv_w, preferred_element_type=F32)
    queries = turn_heads(to_heads(linear[:, :q_width], q_heads), cosine_table, sine_values)
    queries = queries.astype(BF16)
    keys = turn_heads(
        to_heads(linear[:, q_width : q_width + kv_width], kv_heads), cosine_table, sine_values
    ).astype(BF16)
    values = to_heads(linear[:, q_width + kv_width :].astype(BF16), kv_heads)
    mix_heads, totals = attend_forward(queries, keys, values, segments, scale)
    mixed = from_heads(mix_heads)
    all_mixed = lax.all_gather(mixed, "tensor", axis=1, tiled=True)
    hidden = inputs + dot_nt(all_mixed, out_w_t)
    normed_moe, factor_m = rms_forward(hidden, gain_m)
    low_moe = normed_moe.astype(BF16)

    logits = jnp.dot(low_moe, router, preferred_element_type=F32)
    expert_ids = jnp.arange(E, dtype=jnp.int32)
    chosen = jnp.any(all_routes[:, :, None] == expert_ids[None, None, :], axis=1)
    peak = jnp.max(jnp.where(chosen, logits, MASKED_SCORE), axis=-1, keepdims=True)
    powers = jnp.where(chosen, jnp.exp(jnp.where(chosen, logits - peak, 0.0)), 0.0)
    gates = powers / jnp.sum(powers, axis=-1, keepdims=True)

    first_expert = member * local_experts
    mine = lax.dynamic_slice_in_dim(chosen, first_expert, local_experts, 1)
    mine = mine.reshape(groups, row_total, local_experts)
    my_gates = lax.dynamic_slice_in_dim(gates, first_expert, local_experts, 1)
    my_gates = my_gates.reshape(groups, row_total, local_experts).transpose(0, 2, 1)
    lower = jnp.tril(jnp.ones((row_total, row_total), BF16))
    rank = jnp.einsum("tu,sue->set", lower, mine.astype(BF16), preferred_element_type=F32)
    place = jnp.where(mine.transpose(0, 2, 1), rank.astype(jnp.int32) - 1, -1)
    slots = jnp.arange(capacity, dtype=jnp.int32)
    named = place[:, :, None, :] == slots[None, None, :, None]
    slot_gate = jnp.sum(jnp.where(named, my_gates[:, :, None, :], 0.0), axis=-1)
    onehot = named.astype(BF16).reshape(groups, local_experts * capacity, row_total)
    slot_rows = groups * capacity

    def dispatch(rows):
        picked = jnp.einsum(
            "sct,std->scd",
            onehot,
            rows.reshape(groups, row_total, width),
            preferred_element_type=F32,
        ).astype(BF16)
        picked = picked.reshape(groups, local_experts, capacity, width)
        return picked.transpose(1, 0, 2, 3).reshape(local_experts, slot_rows, width)

    def combine(rows):
        rows = rows.reshape(local_experts, groups, capacity, width).transpose(1, 0, 2, 3)
        rows = rows.reshape(groups, local_experts * capacity, width)
        return jnp.einsum("sct,scd->std", onehot, rows, preferred_element_type=F32).reshape(
            length, width
        )

    received = dispatch(low_moe)
    grad_rows = dispatch(all_cotangent)
    gate_rows = slot_gate.transpose(1, 0, 2).reshape(local_experts, slot_rows, 1)
    pre_gate = jnp.einsum("erd,edf->erf", received, gate_w, preferred_element_type=F32)
    pre_up = jnp.einsum("erd,edf->erf", received, up_w, preferred_element_type=F32)
    sigmoid_gate = jax.nn.sigmoid(pre_gate)
    silu_gate = pre_gate * sigmoid_gate
    activation = (silu_gate * pre_up).astype(BF16)
    expert_out = jnp.einsum("erf,edf->erd", activation, down_w, preferred_element_type=F32)
    expert_out = expert_out.astype(BF16).astype(F32)
    slot_grad = jnp.sum(grad_rows.astype(F32) * expert_out, axis=-1)
    slot_grad = slot_grad.reshape(local_experts, groups, capacity).transpose(1, 0, 2)
    my_gate_grad = jnp.sum(jnp.where(named, slot_grad[:, :, :, None], 0.0), axis=2)
    my_gate_grad = my_gate_grad.transpose(0, 2, 1).reshape(length, local_experts)
    moe_part = combine((gate_rows * expert_out).astype(BF16)).astype(BF16)
    moe_own = lax.psum_scatter(moe_part, "tensor", scatter_dimension=0, tiled=True)
    own_start = member * row_total
    hidden_own = lax.dynamic_slice_in_dim(hidden, own_start, row_total, 0)
    mixed_out = (hidden_own + moe_own.astype(F32)).astype(BF16)

    out_grad = (gate_rows * grad_rows.astype(F32)).astype(BF16)
    act_grad = jnp.einsum("erd,edf->erf", out_grad, down_w, preferred_element_type=F32)
    gate_grad = (act_grad * pre_up * sigmoid_gate * (1.0 + pre_gate * (1.0 - sigmoid_gate))).astype(
        BF16
    )
    up_grad = (act_grad * silu_gate).astype(BF16)
    row_grad = jnp.einsum("erf,edf->erd", gate_grad, gate_w, preferred_element_type=F32)
    row_grad = row_grad + jnp.einsum("erf,edf->erd", up_grad, up_w, preferred_element_type=F32)
    norm_part = combine(row_grad.astype(BF16)).astype(BF16)
    placed_grad = lax.dynamic_update_slice_in_dim(
        jnp.zeros((length, E), F32), my_gate_grad, first_expert, 1
    )
    high = lax.reduce_precision(placed_grad, 8, 7)
    sides = jnp.concatenate(
        [high.astype(BF16), (placed_grad - high).astype(BF16), jnp.zeros((length, 64), BF16)],
        axis=1,
    )
    joined = jnp.concatenate([norm_part, sides], axis=1)
    joined, gate_grad, up_grad, activation, out_grad = lax.optimization_barrier(
        (joined, gate_grad, up_grad, activation, out_grad)
    )
    joined = lax.psum(joined, "tensor").astype(F32)
    gate_w_grad = jnp.einsum("erd,erf->edf", received, gate_grad, preferred_element_type=F32)
    gate_share = lax.psum_scatter(
        gate_w_grad.astype(BF16), "dp", scatter_dimension=1, tiled=True
    ).astype(F32)
    up_w_grad = jnp.einsum("erd,erf->edf", received, up_grad, preferred_element_type=F32)
    up_share = lax.psum_scatter(
        up_w_grad.astype(BF16), "dp", scatter_dimension=1, tiled=True
    ).astype(F32)
    down_w_grad = jnp.einsum("erd,erf->edf", out_grad, activation, preferred_element_type=F32)
    down_share = lax.psum_scatter(
        down_w_grad.astype(BF16), "dp", scatter_dimension=1, tiled=True
    ).astype(F32)
    down_share = down_share.transpose(0, 2, 1)

    all_gate_grad = joined[:, width : width + E] + joined[:, width + E : width + 2 * E]
    logit_grad = gates * (all_gate_grad - jnp.sum(gates * all_gate_grad, axis=-1, keepdims=True))
    norm_moe_grad = joined[:, :width] + jnp.dot(
        logit_grad, router.astype(F32).T, precision=HIGHEST
    )
    logit_high = lax.reduce_precision(logit_grad, 8, 7)
    logit_pair = jnp.concatenate(
        [logit_high.astype(BF16), (logit_grad - logit_high).astype(BF16)], axis=1
    )
    router_pair = dot_tn(low_moe, logit_pair)
    router_grad = router_pair[:, :E] + router_pair[:, E:]
    hidden_back, gain_m_grad = rms_backward(hidden, factor_m, gain_m, norm_moe_grad)
    hidden_grad = all_cotangent.astype(F32) + hidden_back
    branch_grad = hidden_grad.astype(BF16)
    hidden_grad_own = lax.dynamic_slice_in_dim(hidden_grad, own_start, row_total, 0)

    out_w_grad = dot_tn(branch_grad, mixed)
    my_out_w = lax.dynamic_slice_in_dim(out_w_t, member * q_width, q_width, 1)
    mix_grad = jnp.dot(branch_grad, my_out_w, preferred_element_type=F32).astype(BF16)
    query_grad, key_grad, value_grad = attend_backward(
        queries, keys, values, segments, totals, mix_heads, to_heads(mix_grad, q_heads), scale
    )
    linear_grad = jnp.concatenate(
        [
            from_heads(turn_heads(query_grad, cosine_table, -sine_values).astype(BF16)),
            from_heads(turn_heads(key_grad, cosine_table, -sine_values).astype(BF16)),
            from_heads(value_grad.astype(BF16)),
        ],
        axis=1,
    )
    qkv_w_grad = dot_tn(normed, linear_grad)
    summed = dot_nt(linear_grad, qkv_w)
    gain_a_grad = jnp.sum(summed * (inputs * factor_a), axis=0)
    side_grads = jnp.concatenate(
        [router_grad, gain_m_grad[:, None], gain_a_grad[:, None], jnp.zeros((width, 94), F32)],
        axis=1,
    )
    weight_grads = jnp.concatenate([qkv_w_grad, out_w_grad, side_grads], axis=1).astype(BF16)
    shares = lax.psum_scatter(weight_grads, "dp", scatter_dimension=0, tiled=True)
    side_start = qkv_width + q_width
    gain_a_block = shares[:, side_start + E + 1].reshape(groups, 1, gain_part)
    gain_a_block = jnp.pad(gain_a_block, ((0, 0), (0, 15), (0, width - gain_part)))
    summed = jnp.concatenate(
        [summed.astype(BF16).reshape(groups, row_total, width), gain_a_block], axis=1
    ).reshape(groups * (row_total + 16), width)
    reduced = lax.psum_scatter(summed, "tensor", scatter_dimension=0, tiled=True).astype(F32)
    gain_a_share = reduced[row_total, :gain_part]
    norm_attn_grad = reduced[:row_total]
    inputs_own = tokens.astype(F32)
    factor_own = lax.rsqrt(jnp.mean(inputs_own * inputs_own, axis=-1, keepdims=True) + EPSILON)
    input_back, _ = rms_backward(inputs_own, factor_own, gain_a, norm_attn_grad)
    input_grad = hidden_grad_own + input_back
    shares = shares.astype(F32)
    mine_small = lax.dynamic_slice_in_dim(
        shares[:, side_start : side_start + E + 1], member * gain_part, gain_part, 0
    )
    return (
        mixed_out,
        input_grad,
        gain_a_share,
        shares[:, :q_width],
        shares[:, q_width : q_width + kv_width],
        shares[:, q_width + kv_width : qkv_width],
        shares[:, qkv_width:side_start].T,
        mine_small[:, E],
        mine_small[:, :E],
        gate_share,
        up_share,
        down_share,
    )


def solution(mesh):
    placed = (
        P(("dp", "tensor"), None),
        P(("dp", "tensor"), None),
        P("dp"),
        P(("dp", "tensor"), None),
        P(("dp", "tensor")),
        P("dp", "tensor"),
        P("dp", "tensor"),
        P("dp", "tensor"),
        P("tensor", "dp"),
        P(("dp", "tensor")),
        P(("dp", "tensor"), None),
        P("tensor", "dp", None),
        P("tensor", "dp", None),
        P("tensor", None, "dp"),
    )
    return jax.shard_map(
        per_device,
        mesh=mesh,
        in_specs=placed,
        out_specs=(
            P(("dp", "tensor"), None),
            P(("dp", "tensor"), None),
            P(("dp", "tensor")),
            P("dp", "tensor"),
            P("dp", "tensor"),
            P("dp", "tensor"),
            P("tensor", "dp"),
            P(("dp", "tensor")),
            P(("dp", "tensor"), None),
            P("tensor", "dp", None),
            P("tensor", "dp", None),
            P("tensor", None, "dp"),
        ),
        check_vma=False,
    )
```
